256 devices in a mesh: fv: 32 (over x_lo, z, core), tok: 8 (over y, x_hi).
Axes of the slice: x: 4 (x_hi: 2, x_lo: 2; x = x_hi * 2 + x_lo), y: 4, z: 8, core: 2. Of those that a mesh axis runs over, the one named last changes fastest.
Arguments:
- queries: bfloat16 [96, 1024, 1536], P('fv', 'tok'), may hold values from -6 to 6
- keys: bfloat16 [96, 1024, 1536], P('fv', 'tok'), may hold values from -6 to 6
- values: bfloat16 [96, 1024, 1536], P('fv', 'tok'), may hold values from -6 to 6
- adjacency: int32 [6, 2], replicated, may hold values from 0 to 5, as said below
Outputs:
- attended: bfloat16 [96, 1024, 1536], P('fv', 'tok')
The draws below stay inside these ranges and needn't reach their ends.
Inputs may be any that keep to these rules, and one draw needn't show every extreme that they name: `adjacency`: row v holds the left and the right neighbour of camera v on one cycle through all 6 cameras.
All inputs are finite; a program needn't handle non-finite values.
Results may differ from the reference program's by a relative error of at most 0.0049.
Values may be sent and summed in bfloat16 or wider, within the bound.
A program may use at most 128 MiB of HBM per device.

```python
import jax
import jax.numpy as jnp
from jax import lax

VIEWS = 6
HEAD_DIM = 64
WIN = 128
TOK_DEV = 128
D = 1536
FRAMES = 16
PAIRS = 96
TOKENS = 1024
N_TOK = 8


def base_field(key):
    return jnp.clip(jax.random.normal(key, (PAIRS, TOKENS, D), jnp.float32), -6.0, 6.0)


def draw_queries(key, part):
    key = jax.random.fold_in(key, 1)
    field = base_field(key)
    return field.astype(jnp.bfloat16)


def draw_keys(key, part):
    key = jax.random.fold_in(key, 2)
    field = base_field(key)
    return field.astype(jnp.bfloat16)


def draw_adjacency(key, part):
    key = jax.random.fold_in(key, 3)
    cycle = jax.random.permutation(key, VIEWS).astype(jnp.int32)
    position = jnp.argsort(cycle).astype(jnp.int32)
    leftward = cycle[(position - 1) % VIEWS]
    rightward = cycle[(position + 1) % VIEWS]
    return jnp.stack([leftward, rightward], axis=1).astype(jnp.int32)


def shard_levels(rng, dims, shards, low, largest):
    def one(dim, blocks):
        steps = jax.random.uniform(jax.random.fold_in(jax.random.fold_in(rng, 6), dim), (blocks,), jnp.float32, low / len(shards), largest / len(shards))
        return jnp.repeat(jnp.exp(steps), dims[dim] // blocks).reshape((-1,) + (1,) * (len(dims) - dim - 1))

    level = one(*shards[0])
    for cut in shards[1:]:
        level = level * one(*cut)
    return level


def centred(own_key, shape, width, most, cuts=(), held_as=jnp.bfloat16):
    result = jax.random.normal(own_key, shape, jnp.float32) * width
    if len(cuts) > 0:
        result = shard_levels(own_key, shape, cuts, -0.22, 0.18) * result
    return jnp.clip(result, min=-most, max=most).astype(held_as)


def setup_inputs(seed: int = 0) -> dict:
    streams_of = jax.random.split(jax.random.key(seed), 5)
    queries = draw_queries(jax.random.fold_in(streams_of[4], 71), 0)
    keys = draw_keys(jax.random.fold_in(streams_of[4], 71), 0)
    values = centred(streams_of[2], (PAIRS, TOKENS, D), 1.0, 6.0, ((0, 32), (1, 8)))
    adjacency = draw_adjacency(jax.random.fold_in(streams_of[4], 71), 0)
    return dict(queries=queries, keys=keys, values=values, adjacency=adjacency)


def frame_cross(query_frame, key_frame, value_frame, selector):
    width_half = query_frame.shape[-1]
    head_count = width_half // HEAD_DIM
    key_rows = TOK_DEV + 2 * WIN
    stacked = jnp.stack([key_frame, value_frame]).astype(jnp.float32)
    padded = jnp.pad(stacked, ((0, 0), (0, 0), (WIN, WIN), (0, 0)))

    def one_band(block_index):
        start = block_index * TOK_DEV
        query_block = lax.dynamic_slice_in_dim(query_frame, start, TOK_DEV, 1).astype(jnp.float32)
        block_pairs = lax.dynamic_slice_in_dim(padded, start, key_rows, 2)
        chosen = jnp.einsum("wsu,aukc->awskc", selector, block_pairs)
        query_heads = query_block.reshape(VIEWS, TOK_DEV, head_count, HEAD_DIM)
        key_heads = chosen[0].reshape(VIEWS, 3, key_rows, head_count, HEAD_DIM)
        value_heads = chosen[1].reshape(VIEWS, 3, key_rows, head_count, HEAD_DIM)
        scores = jnp.einsum("wthd,wskhd->whtsk", query_heads, key_heads) * (HEAD_DIM ** -0.5)
        query_pos = start + jnp.arange(TOK_DEV, dtype=jnp.int32)
        key_pos = start - WIN + jnp.arange(key_rows, dtype=jnp.int32)
        distance = query_pos[:, None] - key_pos[None, :]
        allowed = (jnp.abs(distance) <= WIN) & (key_pos >= 0)[None, :] & (key_pos < TOKENS)[None, :]
        scores = jnp.where(allowed[None, None, :, None, :], scores, -jnp.inf)
        row_max = jnp.max(scores, axis=(3, 4), keepdims=True)
        raised = jnp.exp(scores - row_max)
        denominator = jnp.sum(raised, axis=(3, 4), keepdims=True)
        weights = lax.optimization_barrier((raised / denominator).astype(jnp.bfloat16))
        mixed = jnp.einsum("whtsk,wskhd->wthd", weights.astype(jnp.float32), value_heads)
        return mixed.reshape(VIEWS, TOK_DEV, width_half).astype(jnp.bfloat16)

    bands = lax.map(one_band, jnp.arange(N_TOK, dtype=jnp.int32))
    return jnp.transpose(bands, (1, 0, 2, 3)).reshape(VIEWS, TOKENS, width_half)


def reference(queries, keys, values, adjacency):
    width_half = D // 2
    head_count = width_half // HEAD_DIM
    view_ids = jnp.arange(VIEWS, dtype=jnp.int32)
    picked = jnp.stack([view_ids, adjacency[:, 0], adjacency[:, 1]], axis=1)
    selector = (picked[:, :, None] == view_ids[None, None, :]).astype(jnp.float32)
    cross_query = queries[:, :, :width_half].reshape(FRAMES, VIEWS, TOKENS, width_half)
    cross_key = keys[:, :, :width_half].reshape(FRAMES, VIEWS, TOKENS, width_half)
    cross_value = values[:, :, :width_half].reshape(FRAMES, VIEWS, TOKENS, width_half)
    cross_out = lax.map(lambda items: frame_cross(items[0], items[1], items[2], selector), (cross_query, cross_key, cross_value))
    cross_out = cross_out.reshape(PAIRS, TOKENS, width_half)
    temporal_query = queries[:, :, width_half:].astype(jnp.float32).reshape(FRAMES, VIEWS, TOKENS, head_count, HEAD_DIM)
    temporal_key = keys[:, :, width_half:].astype(jnp.float32).reshape(FRAMES, VIEWS, TOKENS, head_count, HEAD_DIM)
    temporal_value = values[:, :, width_half:].astype(jnp.float32).reshape(FRAMES, VIEWS, TOKENS, head_count, HEAD_DIM)
    scores = jnp.einsum("fvthd,gvthd->vthfg", temporal_query, temporal_key) * (HEAD_DIM ** -0.5)
    row_max = jnp.max(scores, axis=-1, keepdims=True)
    raised = jnp.exp(scores - row_max)
    denominator = jnp.sum(raised, axis=-1, keepdims=True)
    weights = lax.optimization_barrier((raised / denominator).astype(jnp.bfloat16))
    temporal_out = jnp.einsum("vthfg,gvthd->fvthd", weights.astype(jnp.float32), temporal_value)
    temporal_out = temporal_out.reshape(PAIRS, TOKENS, width_half).astype(jnp.bfloat16)
    return jnp.concatenate([cross_out, temporal_out], axis=-1)
```

```python
import jax
import jax.numpy as jnp
from jax import lax
from jax.experimental import pallas as pl
from jax.experimental.pallas import tpu as pltpu
from jax.sharding import PartitionSpec as P

MESH = pl.DeviceIdType.MESH
VIEWS = 6
CAMS = 3
HEAD_DIM = 64
FRAMES = 16
RING = 8
ROWS = 128
HALF = 768
GROUP = 16
COLS = 384
LANES = 128
FAR = -1e30
RATE = HEAD_DIM ** -0.5 * 1.4426950408889634
BF16 = jnp.bfloat16
F32 = jnp.float32


def lane_masks():
    lane = lax.broadcasted_iota(jnp.int32, (1, LANES), 1)
    low = (lane < HEAD_DIM).astype(F32)
    return low.astype(BF16), (1.0 - low).astype(BF16), lane < HEAD_DIM


def scores_of(q, k):
    return lax.dot_general(q, k, (((1,), (1,)), ((), ())), preferred_element_type=F32)


def mix(p, v):
    wide = jnp.concatenate([v, jnp.ones_like(v)], axis=1)
    return lax.dot_general(p, wide, (((1,), (0,)), ((), ())), preferred_element_type=F32)


def kernel(q, k, v, adj, out, qx, ko, vo, kx, vx, ky, vy, tr, ts, tout, co, part, bias_x, bias_y, bias_t,
           load_sem, own_sem, x_send, x_recv, xc_send, xc_recv, y_send, y_recv, yc_send, yc_recv,
           t_send, t_recv, r_send, r_recv, out_sem):
    fv = lax.axis_index("fv")
    tok = lax.axis_index("tok")
    core = fv % 2
    z = (fv // 2) % RING
    xl = fv // (2 * RING)
    xh = tok % 2
    y = tok // 2
    frame = fv // 2

    sibling = (fv + 1 - 2 * core, tok)
    across = (fv, tok + 1 - 2 * xh)
    step = 1 - 2 * xh
    up = (fv, ((y + step + 4) % 4) * 2 + xh)
    down = (fv, ((y - step + 4) % 4) * 2 + xh)

    def peer(dz, dx):
        pz = (z + dz) % RING
        px = (xl + dx) % 2
        return pz, px, (px * 2 * RING + pz * 2 + core, tok)

    peers = [(dz, 0) for dz in (1, 7, 2, 6, 3, 5, 4)] + [(dz, 1) for dz in (0, 1, 7, 2, 6, 3, 5, 4)]
    mine = pl.ds(core * CAMS, CAMS)
    cross_cols = pl.ds(0, HALF)

    local = [
        pltpu.make_async_copy(q.at[:, :, cross_cols], qx, load_sem.at[0]),
        pltpu.make_async_copy(k.at[:, :, cross_cols], ko.at[mine], own_sem.at[0]),
        pltpu.make_async_copy(v.at[:, :, cross_cols], vo.at[mine], own_sem.at[1]),
    ]
    for copy in local:
        copy.start()

    barrier = pltpu.get_barrier_semaphore()
    everyone = [sibling, across, up, down] + [peer(*d)[2] for d in peers]
    for device in everyone:
        pl.semaphore_signal(barrier, inc=1, device_id=device, device_id_type=MESH)
    pl.semaphore_wait(barrier, len(everyone))

    def remote(src, dst, send, recv, device):
        return pltpu.make_async_remote_copy(
            src_ref=src, dst_ref=dst, send_sem=send, recv_sem=recv, device_id=device, device_id_type=MESH)

    own_pairs = [
        remote(k.at[:, :, cross_cols], ko.at[mine], xc_send.at[6], own_sem.at[2], sibling),
        remote(v.at[:, :, cross_cols], vo.at[mine], xc_send.at[7], own_sem.at[3], sibling),
    ]
    for copy in own_pairs:
        copy.start()

    to_across = []
    for c in range(CAMS):
        for a, (src, dst) in enumerate(((k, kx), (v, vx))):
            to_across.append(remote(src.at[c, :, cross_cols], dst.at[core * CAMS + c],
                                    x_send.at[2 * c + a], x_recv.at[2 * c + a], across))
    for copy in to_across:
        copy.start()

    for a, src in enumerate((q, k, v)):
        for c in range(CAMS):
            pltpu.make_async_copy(
                src.at[c, pl.ds(pl.multiple_of(z * GROUP, GROUP), GROUP), pl.ds(pl.multiple_of(HALF + xl * COLS, LANES), COLS)],
                tr.at[c, a, frame], t_recv.at[c]).start()
    for c in range(CAMS):
        for d in peers:
            pz, px, device = peer(*d)
            for a, src in enumerate((q, k, v)):
                remote(
                    src.at[c, pl.ds(pl.multiple_of(pz * GROUP, GROUP), GROUP), pl.ds(pl.multiple_of(HALF + px * COLS, LANES), COLS)],
                    tr.at[c, a, frame], t_send.at[c], t_recv.at[c], device).start()

    row = lax.broadcasted_iota(jnp.int32, (ROWS, ROWS), 0)
    col = lax.broadcasted_iota(jnp.int32, (ROWS, ROWS), 1)
    sign = 1 - 2 * xh
    bias_x[...] = jnp.where((col - row) * sign <= 0, 0.0, FAR).astype(F32)
    inside = jnp.where(xh == 0, y, 3 - y) > 0
    edge = jnp.where(inside, 0, 2 * ROWS)
    bias_y[...] = jnp.where((col - row) * sign >= edge, 0.0, FAR).astype(F32)
    trow = lax.broadcasted_iota(jnp.int32, (FRAMES * GROUP, FRAMES * GROUP), 0)
    tcol = lax.broadcasted_iota(jnp.int32, (FRAMES * GROUP, FRAMES * GROUP), 1)
    bias_t[...] = jnp.where((trow - tcol) % GROUP == 0, 0.0, FAR).astype(F32)

    low, high, is_low = lane_masks()

    def block(kbuf, vbuf, bias, w, cols):
        qv = qx[w, :, cols]
        both = jnp.concatenate([qv * low, qv * high], axis=0)
        view = core * CAMS + w
        cams = (view, adj[view, 0], adj[view, 1])
        s = scores_of(both, jnp.concatenate([kbuf[c, :, cols] for c in cams], axis=0))
        if bias is not None:
            b = bias[...]
            b = jnp.concatenate([b, b, b], axis=1)
            s = s + jnp.concatenate([b, b], axis=0)
        m = jnp.max(s, axis=1, keepdims=True)
        p = jnp.exp2((s - m) * RATE).astype(BF16)
        o = mix(p, jnp.concatenate([vbuf[c, :, cols] for c in cams], axis=0))
        top = jnp.where(is_low, m[:ROWS], m[ROWS:])
        total = jnp.where(is_low, o[:ROWS, LANES:], o[ROWS:, LANES:])
        acc = jnp.where(is_low, o[:ROWS, :LANES], o[ROWS:, :LANES])
        return top, total, acc

    def pass_over(kbuf, vbuf, bias, slot):
        def one(p, _):
            cols = pl.ds(pl.multiple_of(p * LANES, LANES), LANES)
            for w in range(CAMS):
                res = block(kbuf, vbuf, bias, w, cols)
                if slot < 2:
                    for i in range(3):
                        part[slot, i, w, p] = res[i]
                else:
                    tops = [part[0, 0, w, p], part[1, 0, w, p], res[0]]
                    top = jnp.maximum(jnp.maximum(tops[0], tops[1]), tops[2])
                    e = [jnp.exp2((t - top) * RATE) for t in tops]
                    total = part[0, 1, w, p] * e[0] + part[1, 1, w, p] * e[1] + res[1] * e[2]
                    acc = part[0, 2, w, p] * e[0] + part[1, 2, w, p] * e[1] + res[2] * e[2]
                    co[w, :, cols] = (acc / total).astype(BF16)
            return 0
        lax.fori_loop(0, HALF // LANES, one, 0)

    for copy in local:
        copy.wait()
    for copy in own_pairs:
        copy.wait()
    pass_over(ko, vo, None, 0)

    forwards, pairs_x = [], []
    for c in range(CAMS):
        for a, (xb, yb) in enumerate(((kx, ky), (vx, vy))):
            i = 2 * c + a
            to_across[i].wait_recv()
            slot = core * CAMS + c
            f = remote(xb.at[slot], yb.at[slot], y_send.at[i], y_recv.at[i], up)
            f.start()
            forwards.append(f)
            g = remote(xb.at[slot], xb.at[slot], xc_send.at[i], xc_recv.at[i], sibling)
            g.start()
            pairs_x.append(g)
    for g in pairs_x:
        g.wait_recv()
    pass_over(kx, vx, bias_x, 1)

    pairs_y = []
    for c in range(CAMS):
        for a, yb in enumerate((ky, vy)):
            i = 2 * c + a
            forwards[i].wait_recv()
            slot = core * CAMS + c
            g = remote(yb.at[slot], yb.at[slot], yc_send.at[i], yc_recv.at[i], sibling)
            g.start()
            pairs_y.append(g)

    def temporal(c):
        pltpu.make_async_copy(tr.at[c], tr.at[c], t_recv.at[c]).wait()

        def one(p, _):
            cols = pl.ds(pl.multiple_of(p * LANES, LANES), LANES)
            flat = FRAMES * GROUP
            qt, kt, vt = (tr[c, a, :, :, cols].reshape(flat, LANES) for a in range(3))
            res = []
            for mask in (low, high):
                s = scores_of(qt * mask, kt) + bias_t[...]
                m = jnp.max(s, axis=1, keepdims=True)
                o = mix(jnp.exp2((s - m) * RATE).astype(BF16), vt)
                res.append(o[:, :LANES] / o[:, LANES:])
            o = jnp.where(is_low, res[0], res[1]).astype(BF16)
            ts[c, :, :, cols] = o.reshape(FRAMES, GROUP, LANES)
            return 0
        lax.fori_loop(0, COLS // LANES, one, 0)
        place = (c, pl.ds(pl.multiple_of(z * GROUP, GROUP), GROUP), pl.ds(pl.multiple_of(xl * COLS, LANES), COLS))
        pltpu.make_async_copy(ts.at[c, frame], tout.at[place], r_recv.at[c]).start()
        for d in peers:
            pz, px, device = peer(*d)
            remote(ts.at[c, px * RING + pz], tout.at[place], r_send.at[c], r_recv.at[c], device).start()

    for c in range(CAMS):
        temporal(c)

    for g in pairs_y:
        g.wait_recv()
    pass_over(ky, vy, bias_y, 2)
    last = [pltpu.make_async_copy(co, out.at[:, :, cross_cols], out_sem.at[CAMS])]
    last[0].start()
    for c in range(CAMS):
        pltpu.make_async_copy(tout.at[c], tout.at[c], r_recv.at[c]).wait()
        copy = pltpu.make_async_copy(tout.at[c], out.at[c, :, pl.ds(HALF, HALF)], out_sem.at[c])
        copy.start()
        last.append(copy)

    for copy in to_across + forwards + pairs_x + pairs_y:
        copy.wait_send()
    for c in range(CAMS):
        sent = tr.at[c, :, pl.ds(0, FRAMES - 1)]
        pltpu.make_async_copy(sent, sent, t_send.at[c]).wait()
        sent = ts.at[c, pl.ds(0, FRAMES - 1)]
        pltpu.make_async_copy(sent, sent, r_send.at[c]).wait()
    for copy in last:
        copy.wait()


def body(queries, keys, values, adjacency):
    dma = pltpu.SemaphoreType.DMA
    any_spec = pl.BlockSpec(memory_space=pl.ANY)
    six = pltpu.VMEM((VIEWS, ROWS, HALF), BF16)
    three = pltpu.VMEM((CAMS, ROWS, HALF), BF16)
    flat = FRAMES * GROUP
    return pl.pallas_call(
        kernel,
        out_shape=jax.ShapeDtypeStruct(queries.shape, BF16),
        in_specs=[any_spec] * 3 + [pl.BlockSpec(memory_space=pltpu.SMEM)],
        out_specs=any_spec,
        scratch_shapes=[
            three, six, six, six, six, six, six,
            pltpu.VMEM((CAMS, 3, FRAMES, GROUP, COLS), BF16),
            pltpu.VMEM((CAMS, FRAMES, GROUP, COLS), BF16),
            three, three,
            pltpu.VMEM((2, 3, CAMS, HALF // LANES, ROWS, LANES), F32),
            pltpu.VMEM((ROWS, ROWS), F32),
            pltpu.VMEM((ROWS, ROWS), F32),
            pltpu.VMEM((flat, flat), F32),
            dma((1,)), dma((4,)), dma((6,)), dma((6,)), dma((8,)), dma((6,)), dma((6,)), dma((6,)), dma((6,)), dma((6,)),
            dma((3,)), dma((3,)), dma((3,)), dma((3,)), dma((4,)),
        ],
        compiler_params=pltpu.CompilerParams(
            collective_id=0, has_side_effects=True, vmem_limit_bytes=48 << 20),
        cost_estimate=pl.CostEstimate(flops=3_000_000_000, bytes_accessed=5_000_000, transcendentals=7_000_000),
        name="views_and_frames",
    )(queries, keys, values, adjacency)


def solution(mesh):
    in_specs = (P("fv", "tok", None), P("fv", "tok", None), P("fv", "tok", None), P())
    return jax.shard_map(body, mesh=mesh, in_specs=in_specs, out_specs=P("fv", "tok", None), check_vma=False)
```

```python
import jax
import jax.numpy as jnp
from jax import lax
from jax.experimental import pallas as pl
from jax.experimental.pallas import tpu as pltpu
from jax.sharding import PartitionSpec as P

MESH = pl.DeviceIdType.MESH
VIEWS = 6
CAMS = 3
HEAD_DIM = 64
FRAMES = 16
RING = 8
ROWS = 128
HALF = 768
GROUP = 16
COLS = 384
LANES = 128
FAR = -1e30
RATE = HEAD_DIM ** -0.5 * 1.4426950408889634
BF16 = jnp.bfloat16
F32 = jnp.float32
GROUPS = 6
DIRECT = (2,)


def lane_masks():
    lane = lax.broadcasted_iota(jnp.int32, (1, LANES), 1)
    low = (lane < HEAD_DIM).astype(F32)
    return low.astype(BF16), (1.0 - low).astype(BF16), lane < HEAD_DIM


def scores_of(q, k):
    return lax.dot_general(q, k, (((1,), (1,)), ((), ())), preferred_element_type=F32)


def mix(p, v):
    wide = jnp.concatenate([v, jnp.ones_like(v)], axis=1)
    return lax.dot_general(p, wide, (((1,), (0,)), ((), ())), preferred_element_type=F32)


def kernel(q, k, v, adj, out_c, out_t, qx, ko, vo, kx, vx, ky, vy, tr, ts, co, lo, rb, part, bias_x, bias_y, bias_t,
           load_sem, own_sem, own_send, x_send, x_recv, xc_send, xc_recv, y_send, y_recv, yc_send, yc_recv,
           t_send, t_recv, r_send, r_recv, lo_send, lo_recv, rb_recv, rx_send, rx_recv, out_sem):
    fv = lax.axis_index("fv")
    tok = lax.axis_index("tok")
    core = fv % 2
    z = (fv // 2) % RING
    xl = fv // (2 * RING)
    xh = tok % 2
    y = tok // 2
    frame = fv // 2

    sibling = (fv + 1 - 2 * core, tok)
    across = (fv, tok + 1 - 2 * xh)
    step = 1 - 2 * xh
    up = (fv, ((y + step + 4) % 4) * 2 + xh)
    down = (fv, ((y - step + 4) % 4) * 2 + xh)

    beside = ((1 - xl) * 2 * RING + z * 2 + core, tok)
    other_frame = (1 - xl) * RING + z

    def peer(dz):
        pz = (z + dz) % RING
        return pz, (xl * 2 * RING + pz * 2 + core, tok)

    peers = (1, 7, 2, 6, 3, 5, 4)
    mine = pl.ds(core * CAMS, CAMS)
    cross_cols = pl.ds(0, HALF)

    local = [
        pltpu.make_async_copy(q.at[:, :, cross_cols], qx, load_sem.at[0]),
        pltpu.make_async_copy(k.at[:, :, cross_cols], ko.at[mine], own_sem.at[0]),
        pltpu.make_async_copy(v.at[:, :, cross_cols], vo.at[mine], own_sem.at[1]),
    ]

    def diagonal(dz):
        pz = (z + dz) % RING
        return pz, ((1 - xl) * 2 * RING + pz * 2 + core, tok)

    barrier = pltpu.get_barrier_semaphore()
    everyone = [sibling, across, beside, up, down] + [peer(d)[1] for d in peers]
    if DIRECT:
        everyone += [diagonal(d)[1] for d in peers]
    for device in everyone:
        pl.semaphore_signal(barrier, inc=1, device_id=device, device_id_type=MESH)
    pl.semaphore_wait(barrier, len(everyone))

    def remote(src, dst, send, recv, device):
        return pltpu.make_async_remote_copy(
            src_ref=src, dst_ref=dst, send_sem=send, recv_sem=recv, device_id=device, device_id_type=MESH)

    own_pairs = [
        remote(k.at[:, :, cross_cols], ko.at[mine], own_send.at[0], own_sem.at[2], sibling),
        remote(v.at[:, :, cross_cols], vo.at[mine], own_send.at[1], own_sem.at[3], sibling),
    ]

    def start_own():
        for copy in local + own_pairs:
            copy.start()

    width = HALF // GROUPS
    to_across = []
    for g in range(GROUPS):
        for a, (src, dst) in enumerate(((k, kx), (v, vx))):
            to_across.append(remote(src.at[:, :, pl.ds(g * width, width)], dst[g].at[mine],
                                    x_send.at[g, a], x_recv.at[g, a], across))

    def across_send(c):
        for copy in to_across[2 * c:2 * c + 2]:
            copy.start()

    def rows_of(pz):
        return pl.ds(pl.multiple_of(pz * GROUP, GROUP), GROUP)

    def half_of(px, start=0):
        return pl.ds(pl.multiple_of(start + px * COLS, LANES), COLS)

    to_beside = [
        [remote(src.at[c, :, half_of(1 - xl, HALF)], lo.at[c, a], lo_send.at[c, a], lo_recv.at[c, a], beside)
         for a, src in enumerate((q, k, v))] for c in range(CAMS)]

    def beside_send(c):
        for copy in to_beside[c]:
            copy.start()

    def own_send(c):
        for a, src in enumerate((q, k, v)):
            pltpu.make_async_copy(src.at[c, rows_of(z), half_of(xl, HALF)], tr.at[c, a, frame], t_recv.at[c]).start()
        for d in peers:
            pz, device = peer(d)
            for a, src in enumerate((q, k, v)):
                remote(src.at[c, rows_of(pz), half_of(xl, HALF)], tr.at[c, a, frame],
                       t_send.at[c], t_recv.at[c], device).start()

    def other_send(c):
        for a in range(3):
            to_beside[c][a].wait_recv()
            pltpu.make_async_copy(lo.at[c, a, rows_of(z)], tr.at[c, a, other_frame], t_recv.at[c]).start()
            for d in peers:
                pz, device = peer(d)
                remote(lo.at[c, a, rows_of(pz)], tr.at[c, a, other_frame],
                       t_send.at[c], t_recv.at[c], device).start()

    row = lax.broadcasted_iota(jnp.int32, (ROWS, ROWS), 0)
    col = lax.broadcasted_iota(jnp.int32, (ROWS, ROWS), 1)
    sign = 1 - 2 * xh
    bias_x[...] = jnp.where((col - row) * sign <= 0, 0.0, FAR).astype(F32)
    inside = jnp.where(xh == 0, y, 3 - y) > 0
    edge = jnp.where(inside, 0, 2 * ROWS)
    bias_y[...] = jnp.where((col - row) * sign >= edge, 0.0, FAR).astype(F32)
    trow = lax.broadcasted_iota(jnp.int32, (FRAMES * GROUP, FRAMES * GROUP), 0)
    tcol = lax.broadcasted_iota(jnp.int32, (FRAMES * GROUP, FRAMES * GROUP), 1)
    bias_t[...] = jnp.where((trow - tcol) % GROUP == 0, 0.0, FAR).astype(F32)

    low, high, is_low = lane_masks()

    def block(kbuf, vbuf, bias, w, cols, inner):
        qv = qx[w, :, cols]
        both = jnp.concatenate([qv * low, qv * high], axis=0)
        view = core * CAMS + w
        cams = (view, adj[0, view], adj[1, view])
        s = scores_of(both, jnp.concatenate([kbuf[c, :, inner] for c in cams], axis=0))
        if bias is not None:
            b = bias[...]
            b = jnp.concatenate([b, b, b], axis=1)
            s = s + jnp.concatenate([b, b], axis=0)
        m = jnp.max(s, axis=1, keepdims=True)
        p = jnp.exp2((s - m) * RATE).astype(BF16)
        o = mix(p, jnp.concatenate([vbuf[c, :, inner] for c in cams], axis=0))
        top = jnp.where(is_low, m[:ROWS], m[ROWS:])
        total = jnp.where(is_low, o[:ROWS, LANES:], o[ROWS:, LANES:])
        acc = jnp.where(is_low, o[:ROWS, :LANES], o[ROWS:, :LANES])
        return top, total, acc

    def pass_over(kbuf, vbuf, bias, slot, g=0, groups=1):
        per = HALF // LANES // groups

        def one(i, _):
            p = g * per + i
            cols = pl.ds(pl.multiple_of(p * LANES, LANES), LANES)
            inner = pl.ds(pl.multiple_of(i * LANES, LANES), LANES)
            found = [block(kbuf, vbuf, bias, w, cols, inner) for w in range(CAMS)]
            for w, res in enumerate(found):
                if slot < 2:
                    for i in range(3):
                        part[slot, i, w, p] = res[i]
                else:
                    tops = [part[0, 0, w, p], part[1, 0, w, p], res[0]]
                    top = jnp.maximum(jnp.maximum(tops[0], tops[1]), tops[2])
                    e = [jnp.exp2((t - top) * RATE) for t in tops]
                    total = part[0, 1, w, p] * e[0] + part[1, 1, w, p] * e[1] + res[1] * e[2]
                    acc = part[0, 2, w, p] * e[0] + part[1, 2, w, p] * e[1] + res[2] * e[2]
                    co[w, :, cols] = (acc / total).astype(BF16)
            return 0
        if per == 1:
            one(0, 0)
        else:
            lax.fori_loop(0, per, one, 0)

    def temporal(c):
        pltpu.make_async_copy(tr.at[c], tr.at[c], t_recv.at[c]).wait()

        def one(p, _):
            cols = pl.ds(pl.multiple_of(p * LANES, LANES), LANES)
            flat = FRAMES * GROUP
            qt, kt, vt = (tr[c, a, :, :, cols].reshape(flat, LANES) for a in range(3))
            res = []
            for mask in (low, high):
                s = scores_of(qt * mask, kt) + bias_t[...]
                m = jnp.max(s, axis=1, keepdims=True)
                o = mix(jnp.exp2((s - m) * RATE).astype(BF16), vt)
                res.append(o[:, :LANES] / o[:, LANES:])
            o = jnp.where(is_low, res[0], res[1]).astype(BF16)
            ts[c, :, :, cols] = o.reshape(FRAMES, GROUP, LANES)
            return 0
        lax.fori_loop(0, COLS // LANES, one, 0)
        place = (c, rows_of(z), half_of(xl))
        pltpu.make_async_copy(ts.at[c, frame], out_t.at[place], r_recv.at[c]).start()
        if c in DIRECT:
            for d in peers:
                pz, device = diagonal(d)
                remote(ts.at[c, (1 - xl) * RING + pz], out_t.at[place], r_send.at[c], rx_recv.at[c], device).start()
                pz, device = peer(d)
                remote(ts.at[c, xl * RING + pz], out_t.at[place], r_send.at[c], r_recv.at[c], device).start()
            remote(ts.at[c, other_frame], out_t.at[place], rx_send.at[c], rx_recv.at[c], beside).start()
            return
        pltpu.make_async_copy(ts.at[c, other_frame], rb.at[c, rows_of(z)], rb_recv.at[c]).start()
        for d in peers:
            pz, device = peer(d)
            remote(ts.at[c, xl * RING + pz], out_t.at[place], r_send.at[c], r_recv.at[c], device).start()
            remote(ts.at[c, (1 - xl) * RING + pz], rb.at[c, rows_of(z)], r_send.at[c], rb_recv.at[c], device).start()

    back = [remote(rb.at[c], out_t.at[c, :, half_of(xl)], rx_send.at[c], rx_recv.at[c], beside) for c in range(CAMS)]

    def relay(c):
        if c in DIRECT:
            return
        pltpu.make_async_copy(rb.at[c], rb.at[c], rb_recv.at[c]).wait()
        back[c].start()

    def pass_own():
        for copy in local:
            copy.wait()
        for copy in own_pairs:
            copy.wait()
        pass_over(ko, vo, None, 0)

    forwards, pairs_x, pairs_y = {}, {}, {}

    def forward_x(g):
        for a, (xb, yb) in enumerate(((kx, ky), (vx, vy))):
            to_across[2 * g + a].wait_recv()
            forwards[g, a] = remote(xb[g].at[mine], yb[g].at[mine], y_send.at[g, a], y_recv.at[g, a], up)
            forwards[g, a].start()
            pairs_x[g, a] = remote(xb[g].at[mine], xb[g].at[mine], xc_send.at[g, a], xc_recv.at[g, a], sibling)
            pairs_x[g, a].start()

    def pass_x(g):
        for a in range(2):
            pairs_x[g, a].wait_recv()
        pass_over(kx[g], vx[g], bias_x, 1, g, GROUPS)

    def forward_y(g):
        for a, yb in enumerate((ky, vy)):
            forwards[g, a].wait_recv()
            pairs_y[g, a] = remote(yb[g].at[mine], yb[g].at[mine], yc_send.at[g, a], yc_recv.at[g, a], sibling)
            pairs_y[g, a].start()

    def pass_y(g):
        for a in range(2):
            pairs_y[g, a].wait_recv()
        pass_over(ky[g], vy[g], bias_y, 2, g, GROUPS)
        here = (slice(None), slice(None), pl.ds(g * width, width))
        last.append(pltpu.make_async_copy(co.at[here], out_c.at[here], out_sem.at[g]))
        last[-1].start()

    last = []
    beside_send(0)
    own_send(0)
    start_own()
    beside_send(1)
    own_send(1)
    beside_send(2)
    own_send(2)
    pass_own()
    other_send(0)
    across_send(0)
    across_send(1)
    other_send(1)
    across_send(2)
    across_send(3)
    other_send(2)
    across_send(4)
    across_send(5)
    forward_x(0)
    forward_x(1)
    temporal(0)
    pass_x(0)
    pass_x(1)
    forward_y(0)
    forward_x(2)
    forward_y(1)
    pass_y(0)
    temporal(1)
    forward_x(3)
    pass_x(2)
    pass_x(3)
    forward_y(2)
    pass_y(1)
    forward_x(4)
    pass_y(2)
    temporal(2)
    pass_x(4)
    forward_y(3)
    forward_x(5)
    pass_x(5)
    pass_y(3)
    relay(0)
    forward_y(4)
    pass_y(4)
    relay(1)
    forward_y(5)
    pass_y(5)

    for copy in to_across + sum(to_beside, []) + [*forwards.values(), *pairs_x.values(), *pairs_y.values()]:
        copy.wait_send()
    for c in range(CAMS):
        sent = tr.at[c, :, pl.ds(0, FRAMES - 2)]
        pltpu.make_async_copy(sent, sent, t_send.at[c]).wait()
        sent = ts.at[c, pl.ds(0, FRAMES - 2)]
        pltpu.make_async_copy(sent, sent, r_send.at[c]).wait()
        if c in DIRECT:
            pltpu.make_async_copy(ts.at[c, 0], ts.at[c, 0], rx_send.at[c]).wait()
        else:
            back[c].wait_send()
        for half, sem in ((xl, r_recv), (1 - xl, rx_recv)):
            here = out_t.at[c, :, half_of(half)]
            pltpu.make_async_copy(here, here, sem.at[c]).wait()
    for copy in last:
        copy.wait()


def body(queries, keys, values, adjacency):
    dma = pltpu.SemaphoreType.DMA
    any_spec = pl.BlockSpec(memory_space=pltpu.HBM)
    six = pltpu.VMEM((VIEWS, ROWS, HALF), BF16)
    three = pltpu.VMEM((CAMS, ROWS, HALF), BF16)
    flat = FRAMES * GROUP
    cross, temporal = pl.pallas_call(
        kernel,
        out_shape=[jax.ShapeDtypeStruct((CAMS, ROWS, HALF), BF16)] * 2,
        in_specs=[any_spec] * 3 + [pl.BlockSpec(memory_space=pltpu.SMEM)],
        out_specs=[any_spec] * 2,
        scratch_shapes=[
            three, six, six, *[[pltpu.VMEM((VIEWS, ROWS, HALF // GROUPS), BF16)] * GROUPS] * 4,
            pltpu.VMEM((CAMS, 3, FRAMES, GROUP, COLS), BF16),
            pltpu.VMEM((CAMS, FRAMES, GROUP, COLS), BF16),
            three,
            pltpu.VMEM((CAMS, 3, ROWS, COLS), BF16),
            pltpu.VMEM((CAMS, ROWS, COLS), BF16),
            pltpu.VMEM((2, 3, CAMS, HALF // LANES, ROWS, LANES), F32),
            pltpu.VMEM((ROWS, ROWS), F32),
            pltpu.VMEM((ROWS, ROWS), F32),
            pltpu.VMEM((flat, flat), F32),
            dma((1,)), dma((4,)), dma((2,)), *[dma((GROUPS, 2))] * 8,
            dma((3,)), dma((3,)), dma((3,)), dma((3,)),
            dma((3, 3)), dma((3, 3)), dma((3,)), dma((3,)), dma((3,)), dma((GROUPS,)),
        ],
        compiler_params=pltpu.CompilerParams(
            collective_id=0, has_side_effects=True, vmem_limit_bytes=60 << 20),
        cost_estimate=pl.CostEstimate(flops=3_000_000_000, bytes_accessed=5_000_000, transcendentals=7_000_000),
        name="views_and_frames",
    )(queries, keys, values, adjacency.T)
    return jnp.concatenate([cross, temporal], axis=-1)


def solution(mesh):
    in_specs = (P("fv", "tok", None), P("fv", "tok", None), P("fv", "tok", None), P())
    return jax.shard_map(body, mesh=mesh, in_specs=in_specs, out_specs=P("fv", "tok", None), check_vma=False)
```

```python
import jax
import jax.numpy as jnp
from jax import lax
from jax.experimental import pallas as pl
from jax.experimental.pallas import tpu as pltpu
from jax.sharding import PartitionSpec as P

MESH = pl.DeviceIdType.MESH
VIEWS = 6
CAMS = 3
HEAD_DIM = 64
FRAMES = 16
RING = 8
ROWS = 128
HALF = 768
GROUP = 16
COLS = 384
LANES = 128
FAR = -1e30
RATE = HEAD_DIM ** -0.5 * 1.4426950408889634
BF16 = jnp.bfloat16
F32 = jnp.float32
GROUPS = 6
DIRECT = (2,)


def lane_masks():
    lane = lax.broadcasted_iota(jnp.int32, (1, LANES), 1)
    low = (lane < HEAD_DIM).astype(F32)
    return low.astype(BF16), (1.0 - low).astype(BF16), lane < HEAD_DIM


def scores_of(q, k):
    return lax.dot_general(q, k, (((1,), (1,)), ((), ())), preferred_element_type=F32)


def mix(p, v):
    wide = jnp.concatenate([v, jnp.ones_like(v)], axis=1)
    return lax.dot_general(p, wide, (((1,), (0,)), ((), ())), preferred_element_type=F32)


def kernel(q, k, v, adj, out_c, out_t, qx, ko, vo, kx, vx, ky, vy, tr, ts, co, lo, rb, part, bias_x, bias_y, bias_t,
           load_sem, own_sem, own_send, x_send, x_recv, xc_send, xc_recv, y_send, y_recv, yc_send, yc_recv,
           t_send, t_recv, r_send, r_recv, lo_send, lo_recv, rb_recv, rx_send, rx_recv, out_sem):
    fv = lax.axis_index("fv")
    tok = lax.axis_index("tok")
    core = fv % 2
    z = (fv // 2) % RING
    xl = fv // (2 * RING)
    xh = tok % 2
    y = tok // 2
    frame = fv // 2

    sibling = (fv + 1 - 2 * core, tok)
    across = (fv, tok + 1 - 2 * xh)
    step = 1 - 2 * xh
    up = (fv, ((y + step + 4) % 4) * 2 + xh)
    down = (fv, ((y - step + 4) % 4) * 2 + xh)

    beside = ((1 - xl) * 2 * RING + z * 2 + core, tok)
    other_frame = (1 - xl) * RING + z

    def peer(dz):
        pz = (z + dz) % RING
        return pz, (xl * 2 * RING + pz * 2 + core, tok)

    peers = (3, 5, 4, 2, 6, 1, 7)
    mine = pl.ds(core * CAMS, CAMS)
    cross_cols = pl.ds(0, HALF)

    local = [
        pltpu.make_async_copy(q.at[:, :, cross_cols], qx, load_sem.at[0]),
        pltpu.make_async_copy(k.at[:, :, cross_cols], ko.at[mine], own_sem.at[0]),
        pltpu.make_async_copy(v.at[:, :, cross_cols], vo.at[mine], own_sem.at[1]),
    ]

    def diagonal(dz):
        pz = (z + dz) % RING
        return pz, ((1 - xl) * 2 * RING + pz * 2 + core, tok)

    barrier = pltpu.get_barrier_semaphore()
    everyone = [sibling, across, beside, up, down] + [peer(d)[1] for d in peers]
    if DIRECT:
        everyone += [diagonal(d)[1] for d in peers]
    for device in everyone:
        pl.semaphore_signal(barrier, inc=1, device_id=device, device_id_type=MESH)
    pl.semaphore_wait(barrier, len(everyone))

    def remote(src, dst, send, recv, device):
        return pltpu.make_async_remote_copy(
            src_ref=src, dst_ref=dst, send_sem=send, recv_sem=recv, device_id=device, device_id_type=MESH)

    own_pairs = [
        remote(k.at[:, :, cross_cols], ko.at[mine], own_send.at[0], own_sem.at[2], sibling),
        remote(v.at[:, :, cross_cols], vo.at[mine], own_send.at[1], own_sem.at[3], sibling),
    ]

    def start_own():
        for copy in local + own_pairs:
            copy.start()

    width = HALF // GROUPS
    to_across = []
    for g in range(GROUPS):
        for a, (src, dst) in enumerate(((k, kx), (v, vx))):
            to_across.append(remote(src.at[:, :, pl.ds(g * width, width)], dst[g].at[mine],
                                    x_send.at[g, a], x_recv.at[g, a], across))

    def across_send(c):
        for copy in to_across[2 * c:2 * c + 2]:
            copy.start()

    def rows_of(pz):
        return pl.ds(pl.multiple_of(pz * GROUP, GROUP), GROUP)

    def half_of(px, start=0):
        return pl.ds(pl.multiple_of(start + px * COLS, LANES), COLS)

    to_beside = [
        [remote(src.at[c, :, half_of(1 - xl, HALF)], lo.at[c, a], lo_send.at[c, a], lo_recv.at[c, a], beside)
         for a, src in enumerate((q, k, v))] for c in range(CAMS)]

    def beside_send(c):
        for copy in to_beside[c]:
            copy.start()

    def own_send(c):
        for a, src in enumerate((q, k, v)):
            pltpu.make_async_copy(src.at[c, rows_of(z), half_of(xl, HALF)], tr.at[c, a, frame], t_recv.at[c]).start()
        for d in peers:
            pz, device = peer(d)
            for a, src in enumerate((q, k, v)):
                remote(src.at[c, rows_of(pz), half_of(xl, HALF)], tr.at[c, a, frame],
                       t_send.at[c], t_recv.at[c], device).start()

    def other_send(c):
        for a in range(3):
            to_beside[c][a].wait_recv()
            pltpu.make_async_copy(lo.at[c, a, rows_of(z)], tr.at[c, a, other_frame], t_recv.at[c]).start()
            for d in peers:
                pz, device = peer(d)
                remote(lo.at[c, a, rows_of(pz)], tr.at[c, a, other_frame],
                       t_send.at[c], t_recv.at[c], device).start()

    row = lax.broadcasted_iota(jnp.int32, (ROWS, ROWS), 0)
    col = lax.broadcasted_iota(jnp.int32, (ROWS, ROWS), 1)
    sign = 1 - 2 * xh
    bias_x[...] = jnp.where((col - row) * sign <= 0, 0.0, FAR).astype(F32)
    inside = jnp.where(xh == 0, y, 3 - y) > 0
    edge = jnp.where(inside, 0, 2 * ROWS)
    bias_y[...] = jnp.where((col - row) * sign >= edge, 0.0, FAR).astype(F32)
    trow = lax.broadcasted_iota(jnp.int32, (FRAMES * GROUP, FRAMES * GROUP), 0)
    tcol = lax.broadcasted_iota(jnp.int32, (FRAMES * GROUP, FRAMES * GROUP), 1)
    bias_t[...] = jnp.where((trow - tcol) % GROUP == 0, 0.0, FAR).astype(F32)

    low, high, is_low = lane_masks()

    def block(kbuf, vbuf, bias, w, cols, inner):
        qv = qx[w, :, cols]
        both = jnp.concatenate([qv * low, qv * high], axis=0)
        view = core * CAMS + w
        cams = (view, adj[0, view], adj[1, view])
        s = scores_of(both, jnp.concatenate([kbuf[c, :, inner] for c in cams], axis=0))
        if bias is not None:
            b = bias[...]
            b = jnp.concatenate([b, b, b], axis=1)
            s = s + jnp.concatenate([b, b], axis=0)
        m = jnp.max(s, axis=1, keepdims=True)
        p = jnp.exp2((s - m) * RATE).astype(BF16)
        o = mix(p, jnp.concatenate([vbuf[c, :, inner] for c in cams], axis=0))
        top = jnp.where(is_low, m[:ROWS], m[ROWS:])
        total = jnp.where(is_low, o[:ROWS, LANES:], o[ROWS:, LANES:])
        acc = jnp.where(is_low, o[:ROWS, :LANES], o[ROWS:, :LANES])
        return top, total, acc

    def pass_over(kbuf, vbuf, bias, slot, g=0, groups=1):
        per = HALF // LANES // groups

        def one(i, _):
            p = g * per + i
            cols = pl.ds(pl.multiple_of(p * LANES, LANES), LANES)
            inner = pl.ds(pl.multiple_of(i * LANES, LANES), LANES)
            found = [block(kbuf, vbuf, bias, w, cols, inner) for w in range(CAMS)]
            for w, res in enumerate(found):
                if slot < 2:
                    for i in range(3):
                        part[slot, i, w, p] = res[i]
                else:
                    tops = [part[0, 0, w, p], part[1, 0, w, p], res[0]]
                    top = jnp.maximum(jnp.maximum(tops[0], tops[1]), tops[2])
                    e = [jnp.exp2((t - top) * RATE) for t in tops]
                    total = part[0, 1, w, p] * e[0] + part[1, 1, w, p] * e[1] + res[1] * e[2]
                    acc = part[0, 2, w, p] * e[0] + part[1, 2, w, p] * e[1] + res[2] * e[2]
                    co[w, :, cols] = (acc / total).astype(BF16)
            return 0
        if per == 1:
            one(0, 0)
        else:
            lax.fori_loop(0, per, one, 0)

    def temporal(c):
        pltpu.make_async_copy(tr.at[c], tr.at[c], t_recv.at[c]).wait()

        def one(p, _):
            cols = pl.ds(pl.multiple_of(p * LANES, LANES), LANES)
            flat = FRAMES * GROUP
            qt, kt, vt = (tr[c, a, :, :, cols].reshape(flat, LANES) for a in range(3))
            res = []
            for mask in (low, high):
                s = scores_of(qt * mask, kt) + bias_t[...]
                m = jnp.max(s, axis=1, keepdims=True)
                o = mix(jnp.exp2((s - m) * RATE).astype(BF16), vt)
                res.append(o[:, :LANES] / o[:, LANES:])
            o = jnp.where(is_low, res[0], res[1]).astype(BF16)
            ts[c, :, :, cols] = o.reshape(FRAMES, GROUP, LANES)
            return 0
        lax.fori_loop(0, COLS // LANES, one, 0)
        place = (c, rows_of(z), half_of(xl))
        pltpu.make_async_copy(ts.at[c, frame], out_t.at[place], r_recv.at[c]).start()
        if c in DIRECT:
            for d in peers:
                pz, device = diagonal(d)
                remote(ts.at[c, (1 - xl) * RING + pz], out_t.at[place], r_send.at[c], rx_recv.at[c], device).start()
                pz, device = peer(d)
                remote(ts.at[c, xl * RING + pz], out_t.at[place], r_send.at[c], r_recv.at[c], device).start()
            remote(ts.at[c, other_frame], out_t.at[place], rx_send.at[c], rx_recv.at[c], beside).start()
            return
        pltpu.make_async_copy(ts.at[c, other_frame], rb.at[c, rows_of(z)], rb_recv.at[c]).start()
        for d in peers:
            pz, device = peer(d)
            remote(ts.at[c, xl * RING + pz], out_t.at[place], r_send.at[c], r_recv.at[c], device).start()
            remote(ts.at[c, (1 - xl) * RING + pz], rb.at[c, rows_of(z)], r_send.at[c], rb_recv.at[c], device).start()

    back = [remote(rb.at[c], out_t.at[c, :, half_of(xl)], rx_send.at[c], rx_recv.at[c], beside) for c in range(CAMS)]

    def relay(c):
        if c in DIRECT:
            return
        pltpu.make_async_copy(rb.at[c], rb.at[c], rb_recv.at[c]).wait()
        back[c].start()

    def pass_own():
        for copy in local:
            copy.wait()
        for copy in own_pairs:
            copy.wait()
        pass_over(ko, vo, None, 0)

    forwards, pairs_x, pairs_y = {}, {}, {}

    def forward_x(g):
        for a, (xb, yb) in enumerate(((kx, ky), (vx, vy))):
            to_across[2 * g + a].wait_recv()
            forwards[g, a] = remote(xb[g].at[mine], yb[g].at[mine], y_send.at[g, a], y_recv.at[g, a], up)
            forwards[g, a].start()
            pairs_x[g, a] = remote(xb[g].at[mine], xb[g].at[mine], xc_send.at[g, a], xc_recv.at[g, a], sibling)
            pairs_x[g, a].start()

    def pass_x(g):
        for a in range(2):
            pairs_x[g, a].wait_recv()
        pass_over(kx[g], vx[g], bias_x, 1, g, GROUPS)

    def forward_y(g):
        for a, yb in enumerate((ky, vy)):
            forwards[g, a].wait_recv()
            pairs_y[g, a] = remote(yb[g].at[mine], yb[g].at[mine], yc_send.at[g, a], yc_recv.at[g, a], sibling)
            pairs_y[g, a].start()

    def pass_y(g):
        for a in range(2):
            pairs_y[g, a].wait_recv()
        pass_over(ky[g], vy[g], bias_y, 2, g, GROUPS)
        here = (slice(None), slice(None), pl.ds(g * width, width))
        last.append(pltpu.make_async_copy(co.at[here], out_c.at[here], out_sem.at[g]))
        last[-1].start()

    last = []
    beside_send(0)
    beside_send(1)
    beside_send(2)
    own_send(0)
    start_own()
    own_send(1)
    own_send(2)
    across_send(0)
    across_send(1)
    pass_own()
    other_send(0)
    other_send(1)
    across_send(2)
    across_send(3)
    other_send(2)
    across_send(4)
    across_send(5)
    forward_x(0)
    forward_x(1)
    temporal(0)
    pass_x(0)
    forward_y(0)
    pass_x(1)
    forward_x(2)
    forward_y(1)
    temporal(1)
    forward_x(3)
    pass_y(0)
    pass_x(2)
    forward_y(2)
    forward_x(4)
    pass_x(3)
    pass_y(1)
    temporal(2)
    forward_x(5)
    forward_y(3)
    pass_x(4)
    pass_y(2)
    relay(0)
    forward_y(4)
    pass_x(5)
    pass_y(3)
    relay(1)
    forward_y(5)
    pass_y(4)
    pass_y(5)

    for copy in to_across + sum(to_beside, []) + [*forwards.values(), *pairs_x.values(), *pairs_y.values()]:
        copy.wait_send()
    for c in range(CAMS):
        sent = tr.at[c, :, pl.ds(0, FRAMES - 2)]
        pltpu.make_async_copy(sent, sent, t_send.at[c]).wait()
        sent = ts.at[c, pl.ds(0, FRAMES - 2)]
        pltpu.make_async_copy(sent, sent, r_send.at[c]).wait()
        if c in DIRECT:
            pltpu.make_async_copy(ts.at[c, 0], ts.at[c, 0], rx_send.at[c]).wait()
        else:
            back[c].wait_send()
        for half, sem in ((xl, r_recv), (1 - xl, rx_recv)):
            here = out_t.at[c, :, half_of(half)]
            pltpu.make_async_copy(here, here, sem.at[c]).wait()
    for copy in last:
        copy.wait()


def body(queries, keys, values, adjacency):
    dma = pltpu.SemaphoreType.DMA
    any_spec = pl.BlockSpec(memory_space=pltpu.HBM)
    six = pltpu.VMEM((VIEWS, ROWS, HALF), BF16)
    three = pltpu.VMEM((CAMS, ROWS, HALF), BF16)
    flat = FRAMES * GROUP
    cross, temporal = pl.pallas_call(
        kernel,
        out_shape=[jax.ShapeDtypeStruct((CAMS, ROWS, HALF), BF16)] * 2,
        in_specs=[any_spec] * 3 + [pl.BlockSpec(memory_space=pltpu.SMEM)],
        out_specs=[any_spec] * 2,
        scratch_shapes=[
            three, six, six, *[[pltpu.VMEM((VIEWS, ROWS, HALF // GROUPS), BF16)] * GROUPS] * 4,
            pltpu.VMEM((CAMS, 3, FRAMES, GROUP, COLS), BF16),
            pltpu.VMEM((CAMS, FRAMES, GROUP, COLS), BF16),
            three,
            pltpu.VMEM((CAMS, 3, ROWS, COLS), BF16),
            pltpu.VMEM((CAMS, ROWS, COLS), BF16),
            pltpu.VMEM((2, 3, CAMS, HALF // LANES, ROWS, LANES), F32),
            pltpu.VMEM((ROWS, ROWS), F32),
            pltpu.VMEM((ROWS, ROWS), F32),
            pltpu.VMEM((flat, flat), F32),
            dma((1,)), dma((4,)), dma((2,)), *[dma((GROUPS, 2))] * 8,
            dma((3,)), dma((3,)), dma((3,)), dma((3,)),
            dma((3, 3)), dma((3, 3)), dma((3,)), dma((3,)), dma((3,)), dma((GROUPS,)),
        ],
        compiler_params=pltpu.CompilerParams(
            collective_id=0, has_side_effects=True, vmem_limit_bytes=52 << 20),
        cost_estimate=pl.CostEstimate(flops=3_000_000_000, bytes_accessed=5_000_000, transcendentals=7_000_000),
        name="views_and_frames",
    )(queries, keys, values, adjacency.T)
    return jnp.concatenate([cross, temporal], axis=-1)


def solution(mesh):
    in_specs = (P("fv", "tok", None), P("fv", "tok", None), P("fv", "tok", None), P())
    return jax.shard_map(body, mesh=mesh, in_specs=in_specs, out_specs=P("fv", "tok", None), check_vma=False)
```

```python
import jax
import jax.numpy as jnp
from jax import lax
from jax.experimental import pallas as pl
from jax.experimental.pallas import tpu as pltpu
from jax.sharding import PartitionSpec as P

MESH = pl.DeviceIdType.MESH
VIEWS = 6
CAMS = 3
HEAD_DIM = 64
FRAMES = 16
RING = 8
ROWS = 128
HALF = 768
GROUP = 16
COLS = 384
LANES = 128
FAR = -1e30
RATE = HEAD_DIM ** -0.5 * 1.4426950408889634
BF16 = jnp.bfloat16
F32 = jnp.float32
GROUPS = 6
DIRECT = (2,)


def lane_masks():
    lane = lax.broadcasted_iota(jnp.int32, (1, LANES), 1)
    low = (lane < HEAD_DIM).astype(F32)
    return low.astype(BF16), (1.0 - low).astype(BF16), lane < HEAD_DIM


def scores_of(q, k):
    return lax.dot_general(q, k, (((1,), (1,)), ((), ())), preferred_element_type=F32)


def mix(p, v):
    wide = jnp.concatenate([v, jnp.ones_like(v)], axis=1)
    return lax.dot_general(p, wide, (((1,), (0,)), ((), ())), preferred_element_type=F32)


def kernel(q, k, v, adj, out_c, out_t, qx, ko, vo, kx, vx, ky, vy, tr, ts, co, lo, rb, part, bias_x, bias_y, bias_t,
           load_sem, own_sem, own_send, x_send, x_recv, xc_send, xc_recv, y_send, y_recv, yc_send, yc_recv,
           t_send, t_recv, r_send, r_recv, lo_send, lo_recv, rb_recv, rx_send, rx_recv, out_sem):
    fv = lax.axis_index("fv")
    tok = lax.axis_index("tok")
    core = fv % 2
    z = (fv // 2) % RING
    xl = fv // (2 * RING)
    xh = tok % 2
    y = tok // 2
    frame = fv // 2

    sibling = (fv + 1 - 2 * core, tok)
    across = (fv, tok + 1 - 2 * xh)
    step = 1 - 2 * xh
    up = (fv, ((y + step + 4) % 4) * 2 + xh)
    down = (fv, ((y - step + 4) % 4) * 2 + xh)

    beside = ((1 - xl) * 2 * RING + z * 2 + core, tok)
    other_frame = (1 - xl) * RING + z

    def peer(dz):
        pz = (z + dz) % RING
        return pz, (xl * 2 * RING + pz * 2 + core, tok)

    peers = (3, 5, 4, 2, 6, 1, 7)
    mine = pl.ds(core * CAMS, CAMS)
    cross_cols = pl.ds(0, HALF)

    local = [
        pltpu.make_async_copy(q.at[:, :, cross_cols], qx, load_sem.at[0]),
        pltpu.make_async_copy(k.at[:, :, cross_cols], ko.at[mine], own_sem.at[0]),
        pltpu.make_async_copy(v.at[:, :, cross_cols], vo.at[mine], own_sem.at[1]),
    ]

    def diagonal(dz):
        pz = (z + dz) % RING
        return pz, ((1 - xl) * 2 * RING + pz * 2 + core, tok)

    barrier = pltpu.get_barrier_semaphore()
    everyone = [sibling, across, beside, up, down] + [peer(d)[1] for d in peers]
    if DIRECT:
        everyone += [diagonal(d)[1] for d in peers]
    for device in everyone:
        pl.semaphore_signal(barrier, inc=1, device_id=device, device_id_type=MESH)
    pl.semaphore_wait(barrier, len(everyone))

    def remote(src, dst, send, recv, device):
        return pltpu.make_async_remote_copy(
            src_ref=src, dst_ref=dst, send_sem=send, recv_sem=recv, device_id=device, device_id_type=MESH)

    own_pairs = [
        remote(k.at[:, :, cross_cols], ko.at[mine], own_send.at[0], own_sem.at[2], sibling),
        remote(v.at[:, :, cross_cols], vo.at[mine], own_send.at[1], own_sem.at[3], sibling),
    ]

    def start_own():
        for copy in local + own_pairs:
            copy.start()

    width = HALF // GROUPS
    to_across = []
    for g in range(GROUPS):
        for a, (src, dst) in enumerate(((k, kx), (v, vx))):
            to_across.append(remote(src.at[:, :, pl.ds(g * width, width)], dst[g].at[mine],
                                    x_send.at[g, a], x_recv.at[g, a], across))

    def across_send(c):
        for copy in to_across[2 * c:2 * c + 2]:
            copy.start()

    def rows_of(pz):
        return pl.ds(pl.multiple_of(pz * GROUP, GROUP), GROUP)

    def half_of(px, start=0):
        return pl.ds(pl.multiple_of(start + px * COLS, LANES), COLS)

    to_beside = [
        [remote(src.at[c, :, half_of(1 - xl, HALF)], lo.at[c, a], lo_send.at[c, a], lo_recv.at[c, a], beside)
         for a, src in enumerate((q, k, v))] for c in range(CAMS)]

    def beside_send(c):
        for copy in to_beside[c]:
            copy.start()

    def own_send(c):
        for a, src in enumerate((q, k, v)):
            pltpu.make_async_copy(src.at[c, rows_of(z), half_of(xl, HALF)], tr.at[c, a, frame], t_recv.at[c]).start()
        for d in peers:
            pz, device = peer(d)
            for a, src in enumerate((q, k, v)):
                remote(src.at[c, rows_of(pz), half_of(xl, HALF)], tr.at[c, a, frame],
                       t_send.at[c], t_recv.at[c], device).start()

    def other_send(c):
        for a in range(3):
            to_beside[c][a].wait_recv()
            pltpu.make_async_copy(lo.at[c, a, rows_of(z)], tr.at[c, a, other_frame], t_recv.at[c]).start()
            for d in peers:
                pz, device = peer(d)
                remote(lo.at[c, a, rows_of(pz)], tr.at[c, a, other_frame],
                       t_send.at[c], t_recv.at[c], device).start()

    row = lax.broadcasted_iota(jnp.int32, (ROWS, ROWS), 0)
    col = lax.broadcasted_iota(jnp.int32, (ROWS, ROWS), 1)
    sign = 1 - 2 * xh
    bias_x[...] = jnp.where((col - row) * sign <= 0, 0.0, FAR).astype(F32)
    inside = jnp.where(xh == 0, y, 3 - y) > 0
    edge = jnp.where(inside, 0, 2 * ROWS)
    bias_y[...] = jnp.where((col - row) * sign >= edge, 0.0, FAR).astype(F32)
    trow = lax.broadcasted_iota(jnp.int32, (FRAMES * GROUP, FRAMES * GROUP), 0)
    tcol = lax.broadcasted_iota(jnp.int32, (FRAMES * GROUP, FRAMES * GROUP), 1)
    bias_t[...] = jnp.where((trow - tcol) % GROUP == 0, 0.0, FAR).astype(F32)

    low, high, is_low = lane_masks()

    def block(kbuf, vbuf, bias, w, cols, inner):
        qv = qx[w, :, cols]
        both = jnp.concatenate([qv * low, qv * high], axis=0)
        view = core * CAMS + w
        cams = (view, adj[0, view], adj[1, view])
        s = scores_of(both, jnp.concatenate([kbuf[c, :, inner] for c in cams], axis=0))
        if bias is not None:
            b = bias[...]
            b = jnp.concatenate([b, b, b], axis=1)
            s = s + jnp.concatenate([b, b], axis=0)
        m = jnp.max(s, axis=1, keepdims=True)
        p = jnp.exp2((s - m) * RATE).astype(BF16)
        o = mix(p, jnp.concatenate([vbuf[c, :, inner] for c in cams], axis=0))
        top = jnp.where(is_low, m[:ROWS], m[ROWS:])
        total = jnp.where(is_low, o[:ROWS, LANES:], o[ROWS:, LANES:])
        acc = jnp.where(is_low, o[:ROWS, :LANES], o[ROWS:, :LANES])
        return top, total, acc

    def pass_over(kbuf, vbuf, bias, slot, g=0, groups=1):
        per = HALF // LANES // groups

        def one(i, _):
            p = g * per + i
            cols = pl.ds(pl.multiple_of(p * LANES, LANES), LANES)
            inner = pl.ds(pl.multiple_of(i * LANES, LANES), LANES)
            found = [block(kbuf, vbuf, bias, w, cols, inner) for w in range(CAMS)]
            for w, res in enumerate(found):
                if slot < 2:
                    for i in range(3):
                        part[slot, i, w, p] = res[i]
                else:
                    tops = [part[0, 0, w, p], part[1, 0, w, p], res[0]]
                    top = jnp.maximum(jnp.maximum(tops[0], tops[1]), tops[2])
                    e = [jnp.exp2((t - top) * RATE) for t in tops]
                    total = part[0, 1, w, p] * e[0] + part[1, 1, w, p] * e[1] + res[1] * e[2]
                    acc = part[0, 2, w, p] * e[0] + part[1, 2, w, p] * e[1] + res[2] * e[2]
                    co[w, :, cols] = (acc / total).astype(BF16)
            return 0
        if per == 1:
            one(0, 0)
        else:
            lax.fori_loop(0, per, one, 0)

    def temporal(c):
        pltpu.make_async_copy(tr.at[c], tr.at[c], t_recv.at[c]).wait()

        def one(p, _):
            cols = pl.ds(pl.multiple_of(p * LANES, LANES), LANES)
            flat = FRAMES * GROUP
            qt, kt, vt = (tr[c, a, :, :, cols].reshape(flat, LANES) for a in range(3))
            res = []
            for mask in (low, high):
                s = scores_of(qt * mask, kt) + bias_t[...]
                m = jnp.max(s, axis=1, keepdims=True)
                o = mix(jnp.exp2((s - m) * RATE).astype(BF16), vt)
                res.append(o[:, :LANES] / o[:, LANES:])
            o = jnp.where(is_low, res[0], res[1]).astype(BF16)
            ts[c, :, :, cols] = o.reshape(FRAMES, GROUP, LANES)
            return 0
        lax.fori_loop(0, COLS // LANES, one, 0)
        place = (c, rows_of(z), half_of(xl))
        pltpu.make_async_copy(ts.at[c, frame], out_t.at[place], r_recv.at[c]).start()
        if c in DIRECT:
            for d in peers:
                pz, device = diagonal(d)
                remote(ts.at[c, (1 - xl) * RING + pz], out_t.at[place], r_send.at[c], rx_recv.at[c], device).start()
                pz, device = peer(d)
                remote(ts.at[c, xl * RING + pz], out_t.at[place], r_send.at[c], r_recv.at[c], device).start()
            remote(ts.at[c, other_frame], out_t.at[place], rx_send.at[c], rx_recv.at[c], beside).start()
            return
        pltpu.make_async_copy(ts.at[c, other_frame], rb.at[c, rows_of(z)], rb_recv.at[c]).start()
        for d in peers:
            pz, device = peer(d)
            remote(ts.at[c, xl * RING + pz], out_t.at[place], r_send.at[c], r_recv.at[c], device).start()
            remote(ts.at[c, (1 - xl) * RING + pz], rb.at[c, rows_of(z)], r_send.at[c], rb_recv.at[c], device).start()

    back = [remote(rb.at[c], out_t.at[c, :, half_of(xl)], rx_send.at[c], rx_recv.at[c], beside) for c in range(CAMS)]

    def relay(c):
        if c in DIRECT:
            return
        pltpu.make_async_copy(rb.at[c], rb.at[c], rb_recv.at[c]).wait()
        back[c].start()

    def pass_own():
        for copy in local:
            copy.wait()
        for copy in own_pairs:
            copy.wait()
        pass_over(ko, vo, None, 0)

    forwards, pairs_x, pairs_y = {}, {}, {}

    def forward_x(g):
        for a, (xb, yb) in enumerate(((kx, ky), (vx, vy))):
            to_across[2 * g + a].wait_recv()
            forwards[g, a] = remote(xb[g].at[mine], yb[g].at[mine], y_send.at[g, a], y_recv.at[g, a], up)
            forwards[g, a].start()
            pairs_x[g, a] = remote(xb[g].at[mine], xb[g].at[mine], xc_send.at[g, a], xc_recv.at[g, a], sibling)
            pairs_x[g, a].start()

    def pass_x(g):
        for a in range(2):
            pairs_x[g, a].wait_recv()
        pass_over(kx[g], vx[g], bias_x, 1, g, GROUPS)

    def forward_y(g):
        for a, yb in enumerate((ky, vy)):
            forwards[g, a].wait_recv()
            pairs_y[g, a] = remote(yb[g].at[mine], yb[g].at[mine], yc_send.at[g, a], yc_recv.at[g, a], sibling)
            pairs_y[g, a].start()

    def pass_y(g):
        for a in range(2):
            pairs_y[g, a].wait_recv()
        pass_over(ky[g], vy[g], bias_y, 2, g, GROUPS)
        here = (slice(None), slice(None), pl.ds(g * width, width))
        last.append(pltpu.make_async_copy(co.at[here], out_c.at[here], out_sem.at[g]))
        last[-1].start()

    last = []
    own_send(0)
    beside_send(0)
    beside_send(1)
    beside_send(2)
    start_own()
    own_send(1)
    own_send(2)
    across_send(0)
    across_send(1)
    pass_own()
    other_send(0)
    other_send(1)
    across_send(2)
    across_send(3)
    other_send(2)
    across_send(4)
    across_send(5)
    forward_x(0)
    forward_x(1)
    temporal(0)
    pass_x(0)
    forward_y(0)
    pass_x(1)
    forward_x(2)
    forward_y(1)
    temporal(1)
    forward_x(3)
    pass_y(0)
    pass_x(2)
    forward_y(2)
    forward_x(4)
    pass_x(3)
    pass_y(1)
    temporal(2)
    forward_x(5)
    forward_y(3)
    pass_x(4)
    pass_y(2)
    relay(0)
    forward_y(4)
    pass_x(5)
    pass_y(3)
    relay(1)
    forward_y(5)
    pass_y(4)
    pass_y(5)

    for copy in to_across + sum(to_beside, []) + [*forwards.values(), *pairs_x.values(), *pairs_y.values()]:
        copy.wait_send()
    for c in range(CAMS):
        sent = tr.at[c, :, pl.ds(0, FRAMES - 2)]
        pltpu.make_async_copy(sent, sent, t_send.at[c]).wait()
        sent = ts.at[c, pl.ds(0, FRAMES - 2)]
        pltpu.make_async_copy(sent, sent, r_send.at[c]).wait()
        if c in DIRECT:
            pltpu.make_async_copy(ts.at[c, 0], ts.at[c, 0], rx_send.at[c]).wait()
        else:
            back[c].wait_send()
        for half, sem in ((xl, r_recv), (1 - xl, rx_recv)):
            here = out_t.at[c, :, half_of(half)]
            pltpu.make_async_copy(here, here, sem.at[c]).wait()
    for copy in last:
        copy.wait()


def body(queries, keys, values, adjacency):
    dma = pltpu.SemaphoreType.DMA
    any_spec = pl.BlockSpec(memory_space=pltpu.HBM)
    six = pltpu.VMEM((VIEWS, ROWS, HALF), BF16)
    three = pltpu.VMEM((CAMS, ROWS, HALF), BF16)
    flat = FRAMES * GROUP
    cross, temporal = pl.pallas_call(
        kernel,
        out_shape=[jax.ShapeDtypeStruct((CAMS, ROWS, HALF), BF16)] * 2,
        in_specs=[any_spec] * 3 + [pl.BlockSpec(memory_space=pltpu.SMEM)],
        out_specs=[any_spec] * 2,
        scratch_shapes=[
            three, six, six, *[[pltpu.VMEM((VIEWS, ROWS, HALF // GROUPS), BF16)] * GROUPS] * 4,
            pltpu.VMEM((CAMS, 3, FRAMES, GROUP, COLS), BF16),
            pltpu.VMEM((CAMS, FRAMES, GROUP, COLS), BF16),
            three,
            pltpu.VMEM((CAMS, 3, ROWS, COLS), BF16),
            pltpu.VMEM((CAMS, ROWS, COLS), BF16),
            pltpu.VMEM((2, 3, CAMS, HALF // LANES, ROWS, LANES), F32),
            pltpu.VMEM((ROWS, ROWS), F32),
            pltpu.VMEM((ROWS, ROWS), F32),
            pltpu.VMEM((flat, flat), F32),
            dma((1,)), dma((4,)), dma((2,)), *[dma((GROUPS, 2))] * 8,
            dma((3,)), dma((3,)), dma((3,)), dma((3,)),
            dma((3, 3)), dma((3, 3)), dma((3,)), dma((3,)), dma((3,)), dma((GROUPS,)),
        ],
        compiler_params=pltpu.CompilerParams(
            collective_id=0, has_side_effects=True, vmem_limit_bytes=52 << 20),
        cost_estimate=pl.CostEstimate(flops=3_000_000_000, bytes_accessed=5_000_000, transcendentals=7_000_000),
        name="views_and_frames",
    )(queries, keys, values, adjacency.T)
    return jnp.concatenate([cross, temporal], axis=-1)


def solution(mesh):
    in_specs = (P("fv", "tok", None), P("fv", "tok", None), P("fv", "tok", None), P())
    return jax.shard_map(body, mesh=mesh, in_specs=in_specs, out_specs=P("fv", "tok", None), check_vma=False)
```
